32 devices in a mesh: dom: 4 (over y, core), seq: 8 (over z, x).
Axes of the slice: x: 2, y: 2, z: 4, core: 2. Of those that a mesh axis runs over, the one named last changes fastest.
Arguments:
- tokens_x: bfloat16 [8192, 4096], P(('dom', 'seq')), may hold values from -6 to 6
- gate_z: bfloat16 [8192, 4096], P(('dom', 'seq')), may hold values from -6 to 6
- in_b: bfloat16 [8192, 128], P(('dom', 'seq')), may hold values from -6 to 6
- in_c: bfloat16 [8192, 128], P(('dom', 'seq')), may hold values from -0.19921875 to 0.19921875
- log_decay: bfloat16 [8192, 64], P(('dom', 'seq')), may hold values from -1 to 0
- domain_ids: int32 [4, 8, 4], P('dom', 'seq'), may hold values from 0 to 3, each once within a row
- out_weight: bfloat16 [4, 4096, 4096], P('dom', None, 'seq'), may hold values from -0.09375 to 0.09375
- norm_gain: float32 [4, 4096], P('dom'), may hold values from 0.1 to 1.9
- skip_gain: float32 [4, 64], P('dom'), may hold values from 0.5 to 8
Outputs:
- mixed: bfloat16 [4, 2048, 4096], P('dom', 'seq')
The draws below stay inside these ranges and needn't reach their ends.
Inputs may be any that keep to these rules, and one draw needn't show every extreme that they name: Each row of domain_ids names every domain once.
All inputs are finite; a program needn't handle non-finite values.
Results may differ from the reference program's by a relative error of at most 0.0056.
Values may be sent and summed in bfloat16 or wider, within the bound.
A program may use at most 192 MiB of HBM per device.

```python
import math
import jax
import jax.numpy as jnp
from jax import lax

D = 4096
HALF_HEADS = 64
P_SIZE = 64
N = 128
SPAN = 256
TOK_DEV = 256
HP = 4096
SEG = 64
DOMAIN_TOKENS = 2048
TOTAL_TOKENS = 8192
N_DOM = 4
N_SEQ = 8


def draw_log_decay(key, part):
    key_rows = jax.random.split(key, 7)
    fast_share = 0.5
    fast = jax.random.uniform(key_rows[0], (HALF_HEADS,)) < fast_share
    fast_rate = jnp.exp(jax.random.uniform(key_rows[1], (HALF_HEADS,), minval=jnp.log(1.0 / 50.0), maxval=jnp.log(1.0 / 25.0)))
    slow_rate = jax.random.uniform(key_rows[2], (HALF_HEADS,), minval=0.1, maxval=0.6) * 2.302585 / DOMAIN_TOKENS
    decay_speed = jnp.where(fast, fast_rate, slow_rate)
    accelerator_multiple = jnp.exp(jax.random.uniform(key_rows[3], (TOTAL_TOKENS // TOK_DEV, 1), minval=-0.5, maxval=0.4))
    accelerator_multiple = jnp.repeat(accelerator_multiple, TOK_DEV, axis=0)
    approximate_value = jax.random.uniform(key_rows[4], (TOTAL_TOKENS, HALF_HEADS), minval=0.5, maxval=1.5)
    token_group = jax.random.uniform(key_rows[5], (TOTAL_TOKENS, 1)) < 3.0 / DOMAIN_TOKENS
    group_length = jnp.log(jax.random.uniform(key_rows[6], (TOTAL_TOKENS, HALF_HEADS), minval=0.5, maxval=0.8))
    value_rows = -decay_speed[None, :] * accelerator_multiple * approximate_value + jnp.where(token_group, group_length, 0.0)
    return value_rows.astype(jnp.bfloat16)


def block_scale(rng, dims, cuts, least, largest):
    loudness = 1.0
    for axis_at, parts in cuts:
        draws = jax.random.uniform(jax.random.fold_in(jax.random.fold_in(rng, 6), axis_at), (parts,), jnp.float32, least / len(cuts), largest / len(cuts))
        loudness = loudness * jnp.repeat(jnp.exp(draws), dims[axis_at] // parts).reshape((-1,) + (1,) * (len(dims) - 1 - axis_at))
    return loudness


def noise(rng, shape, scale, reach, shards=(), kind=jnp.bfloat16):
    values = jax.random.normal(rng, shape, jnp.float32) * scale
    if len(shards) > 0:
        values = block_scale(rng, shape, shards, -0.22, 0.18) * values
    return jnp.clip(values, min=-reach, max=reach).astype(kind)


def setup_inputs(seed: int = 0) -> dict:
    key_list = jax.random.split(jax.random.key(seed), 10)
    return {
        "tokens_x": noise(key_list[0], (TOTAL_TOKENS, HP), 1.0, 6.0, ((0, 32),)),
        "gate_z": noise(key_list[1], (TOTAL_TOKENS, HP), 1.0, 6.0, ((0, 32),)),
        "in_b": noise(key_list[2], (TOTAL_TOKENS, N), 1.0, 6.0, ((0, 32),)),
        "in_c": noise(key_list[3], (TOTAL_TOKENS, N), 0.03, 0.19921875, ((0, 32),)),
        "log_decay": draw_log_decay(jax.random.fold_in(key_list[9], 71), 0),
        "domain_ids": jax.vmap(lambda own: jax.random.permutation(own, N_DOM))(jax.random.split(key_list[5], N_DOM * N_SEQ)).reshape((N_DOM, N_SEQ, N_DOM)).astype(jnp.int32),
        "out_weight": noise(key_list[6], (N_DOM, HP, D), HP ** -0.5, 0.09375, ((0, 4), (2, 8))),
        "norm_gain": jnp.clip(1.0 + 0.18 * jax.random.normal(key_list[7], (N_DOM, HP), jnp.float32), 0.1, 1.9),
        "skip_gain": jnp.clip(jnp.exp(math.log(8.0) - 2.7725887 * jax.random.uniform(key_list[8], (N_DOM, HALF_HEADS), jnp.float32) ** block_scale(key_list[8], (N_DOM, HALF_HEADS), ((0, 4),), -0.2, 0.2)), 0.5, 8.0),
    }


def stream_order(arr, order):
    width = arr.shape[-1]
    blocks = arr.reshape(N_DOM, N_SEQ, N_DOM, SEG, width)
    picked = jnp.take_along_axis(blocks, order[:, :, :, None, None], axis=2)
    return jnp.transpose(picked, (2, 1, 0, 3, 4)).reshape(N_DOM, DOMAIN_TOKENS, width)

def one_domain(packed):
    xs, zs, bs, cs, ls, weight, gain, skip = packed
    blocks = DOMAIN_TOKENS // SPAN
    xc = xs.reshape(blocks, SPAN, HALF_HEADS, P_SIZE)
    zc = zs.reshape(blocks, SPAN, HP)
    bc = bs.reshape(blocks, SPAN, N)
    cc = cs.reshape(blocks, SPAN, N)
    lc = ls.astype(jnp.float32).reshape(blocks, SPAN, HALF_HEADS)
    rows = jnp.arange(SPAN)
    lower = rows[:, None] >= rows[None, :]

    def step(state, inputs):
        xk, zk, bk, ck, lk = inputs
        cum = jnp.cumsum(lk, axis=0)
        scores = jnp.dot(ck, bk.T, preferred_element_type=jnp.float32)
        diff = cum[:, None, :] - cum[None, :, :]
        decay = jnp.where(lower[:, :, None], jnp.exp(jnp.minimum(diff, 0.0)), 0.0)
        weights = (scores[:, :, None] * decay).astype(jnp.bfloat16)
        inner = jnp.einsum('tuh,uhp->thp', weights.astype(jnp.float32), xk.astype(jnp.float32))
        carried = jnp.einsum('tn,hpn->thp', ck.astype(jnp.float32), state, precision=lax.Precision.HIGHEST)
        ys = inner + jnp.exp(cum)[:, :, None] * carried + skip[None, :, None] * xk.astype(jnp.float32)
        decayed = (xk.astype(jnp.float32) * jnp.exp(cum[-1][None, :] - cum)[:, :, None]).astype(jnp.bfloat16)
        block_state = jnp.einsum('uhp,un->hpn', decayed.astype(jnp.float32), bk.astype(jnp.float32))
        new_state = jnp.exp(cum[-1])[:, None, None] * state + block_state
        gated = ys.reshape(SPAN, HP) * jax.nn.silu(zk.astype(jnp.float32))
        normed = (gated * lax.rsqrt(lax.optimization_barrier(jnp.mean(gated * gated, axis=-1, keepdims=True)) + 1e-05) * gain[None, :]).astype(jnp.bfloat16)
        out = jnp.dot(normed, weight, preferred_element_type=jnp.float32).astype(jnp.bfloat16)
        return (new_state, out)
    start = jnp.zeros((HALF_HEADS, P_SIZE, N), jnp.float32)
    _, outs = lax.scan(step, start, (xc, zc, bc, cc, lc))
    return outs.reshape(DOMAIN_TOKENS, D)

def reference(tokens_x, gate_z, in_b, in_c, log_decay, domain_ids, out_weight, norm_gain, skip_gain):
    order = jnp.argsort(domain_ids, axis=-1).astype(jnp.int32)
    xs = stream_order(tokens_x, order)
    zs = stream_order(gate_z, order)
    bs = stream_order(in_b, order)
    cs = stream_order(in_c, order)
    ls = stream_order(log_decay, order)
    return lax.map(one_domain, (xs, zs, bs, cs, ls, out_weight, norm_gain, skip_gain))
```

```python
import functools

import jax
import jax.numpy as jnp
from jax import lax
from jax.experimental import pallas as pl
from jax.experimental.pallas import tpu as pltpu
from jax.sharding import PartitionSpec as P

BF = jnp.bfloat16
F32 = jnp.float32
PARTNER = 2


def params(**extra):
    return pltpu.CompilerParams(vmem_limit_bytes=48 * 1024 * 1024, **extra)


def exchange(block, axis, bit):
    size = lax.axis_size(axis)
    return lax.ppermute(block, axis, [(i, i ^ bit) for i in range(size)])


def copy_block(order_ref, *refs):
    half = len(refs) // 2
    for src, dst in zip(refs[:half], refs[half:]):
        dst[...] = src[...]


def arrange(order, arrays, groups):
    seg = arrays[0].shape[0] // groups
    return pl.pallas_call(
        copy_block,
        grid_spec=pltpu.PrefetchScalarGridSpec(
            num_scalar_prefetch=1,
            grid=(groups,),
            in_specs=[
                pl.BlockSpec((seg, a.shape[1]), lambda d, o: (o[d], 0)) for a in arrays
            ],
            out_specs=[pl.BlockSpec((seg, a.shape[1]), lambda d, o: (d, 0)) for a in arrays],
        ),
        out_shape=[jax.ShapeDtypeStruct(a.shape, a.dtype) for a in arrays],
        compiler_params=params(),
        name="arrange",
    )(order, *arrays)


def split2(value):
    high = value.astype(BF)
    low = (value - high.astype(F32)).astype(BF)
    return jnp.concatenate([high, low], axis=1)


def spread(heads, lanes, hsize, start):
    row = lax.broadcasted_iota(jnp.int32, (2 * heads, lanes), 0)
    lane = lax.broadcasted_iota(jnp.int32, (2 * heads, lanes), 1) + start
    row = jnp.where(row >= heads, row - heads, row)
    return jnp.where((lane >= row * hsize) & (lane < (row + 1) * hsize), 1.0, 0.0).astype(BF)


def state_kernel(hsize, x_ref, b_ref, l_ref, state_ref, cum_ref, tail, bt):
    rows, heads = l_ref.shape
    lanes = x_ref.shape[1]

    @pl.when(pl.program_id(0) == 0)
    def _():
        t = lax.broadcasted_iota(jnp.int32, (rows, rows), 0)
        u = lax.broadcasted_iota(jnp.int32, (rows, rows), 1)
        lower = jnp.where(t >= u, 1.0, 0.0).astype(BF)
        cum = jnp.dot(lower, l_ref[...], preferred_element_type=F32)
        cum_ref[...] = cum
        tail[...] = split2(jnp.exp(cum[rows - 1 : rows, :] - cum))
        bt[...] = jnp.transpose(b_ref[...].astype(F32)).astype(BF)

    factor = jnp.dot(
        tail[...],
        spread(heads, lanes, hsize, pl.program_id(0) * lanes),
        preferred_element_type=F32,
    )
    decayed = (x_ref[...].astype(F32) * factor).astype(BF)
    state_ref[0] = jnp.dot(bt[...], decayed, preferred_element_type=F32).astype(BF)


def block_states(xs, bs, ls, parts):
    rows, width = xs.shape
    heads, nstate = ls.shape[1], bs.shape[1]
    lanes = width // parts
    return pl.pallas_call(
        functools.partial(state_kernel, width // heads),
        grid=(parts,),
        in_specs=[
            pl.BlockSpec((rows, lanes), lambda j: (0, j)),
            pl.BlockSpec((rows, nstate), lambda j: (0, 0)),
            pl.BlockSpec((rows, heads), lambda j: (0, 0)),
        ],
        out_specs=[
            pl.BlockSpec((1, nstate, lanes), lambda j: (j, 0, 0)),
            pl.BlockSpec((rows, heads), lambda j: (0, 0)),
        ],
        out_shape=[
            jax.ShapeDtypeStruct((parts, nstate, lanes), BF),
            jax.ShapeDtypeStruct((rows, heads), F32),
        ],
        scratch_shapes=[pltpu.VMEM((rows, 2 * heads), BF), pltpu.VMEM((nstate, rows), BF)],
        cost_estimate=pl.CostEstimate(
            flops=2 * rows * width * nstate, bytes_accessed=4 * rows * width, transcendentals=0
        ),
        compiler_params=params(),
        name="block_states",
    )(xs, bs, ls)


def inner_kernel(hsize, x_ref, b_ref, c_ref, cum_ref, cumt_ref, skip_ref, y_ref, scores):
    rows = x_ref.shape[0]
    group = cumt_ref.shape[1]
    half = rows // 2

    @pl.when(pl.program_id(0) == 0)
    def _():
        scores[...] = lax.dot_general(
            c_ref[...], b_ref[...], (((1,), (1,)), ((), ())), preferred_element_type=F32
        )

    lane = lax.broadcasted_iota(jnp.int32, (half, 2 * hsize), 1)

    def product(part, h, x_pair):
        top = part * half
        cols = top + half
        t = lax.broadcasted_iota(jnp.int32, (half, cols), 0) + top
        u = lax.broadcasted_iota(jnp.int32, (half, cols), 1)
        diff = cum_ref[0, top : top + half, h : h + 1] - cumt_ref[0, h : h + 1, :cols]
        decay = jnp.where(t >= u, jnp.exp(jnp.minimum(diff, 0.0)), 0.0)
        weights = (scores[top : top + half, :cols] * decay).astype(BF)
        return jnp.dot(weights, x_pair[:cols], preferred_element_type=F32)

    for pair in range(group // 2):
        at = slice(pair * 2 * hsize, (pair + 1) * 2 * hsize)
        x_pair = x_ref[:, at]
        for part in range(2):
            span = slice(part * half, (part + 1) * half)
            first = product(part, 2 * pair, x_pair)
            second = product(part, 2 * pair + 1, x_pair)
            y_ref[span, at] = (
                jnp.where(lane < hsize, first, second)
                + skip_ref[:, at] * x_pair[span].astype(F32)
            )


def inner_part(xs, bs, cs, cum, skip):
    rows, width = xs.shape
    heads, nstate = cum.shape[1], bs.shape[1]
    steps = heads // 8
    lanes = width // steps
    cum_groups = jnp.transpose(cum.reshape(rows, steps, 8), (1, 0, 2))
    cumt = jnp.transpose(cum_groups, (0, 2, 1))
    return pl.pallas_call(
        functools.partial(inner_kernel, width // heads),
        grid=(steps,),
        in_specs=[
            pl.BlockSpec((rows, lanes), lambda j: (0, j)),
            pl.BlockSpec((rows, nstate), lambda j: (0, 0)),
            pl.BlockSpec((rows, nstate), lambda j: (0, 0)),
            pl.BlockSpec((1, rows, 8), lambda j: (j, 0, 0)),
            pl.BlockSpec((1, 8, rows), lambda j: (j, 0, 0)),
            pl.BlockSpec((1, lanes), lambda j: (0, j)),
        ],
        out_specs=pl.BlockSpec((rows, lanes), lambda j: (0, j)),
        out_shape=jax.ShapeDtypeStruct((rows, width), F32),
        scratch_shapes=[pltpu.VMEM((rows, rows), F32)],
        cost_estimate=pl.CostEstimate(
            flops=16 * rows * rows * width // 4,
            bytes_accessed=40 * rows * width,
            transcendentals=heads * rows * rows,
        ),
        compiler_params=params(),
        name="inner_part",
    )(xs, bs, cs, cum_groups, cumt, skip)


def prefix_kernel(end_ref, total_ref, before_ref):
    parts = end_ref.shape[0]
    running = jnp.zeros(end_ref.shape[1:], F32)
    for s in range(parts):
        before_ref[s] = running.astype(BF)
        if s < parts - 1:
            running = jnp.exp(total_ref[s : s + 1, :]) * running + end_ref[s].astype(F32)


def prefix_states(ends, totals):
    vmem = pl.BlockSpec(memory_space=pltpu.VMEM)
    return pl.pallas_call(
        prefix_kernel,
        in_specs=[vmem, vmem],
        out_specs=vmem,
        out_shape=jax.ShapeDtypeStruct(ends.shape, BF),
        compiler_params=params(),
        name="prefix_states",
    )(ends, totals)


def norm_kernel(hsize, y_ref, z_ref, c_ref, cum_ref, state_ref, gain_ref, out_ref, gated):
    rows, width = y_ref.shape
    heads = cum_ref.shape[1]
    parts, _, lanes = state_ref.shape
    grown = split2(jnp.exp(cum_ref[...]))
    square = jnp.zeros((rows, 1), F32)
    for j in range(parts):
        at = slice(j * lanes, (j + 1) * lanes)
        carried = jnp.dot(c_ref[...], state_ref[j], preferred_element_type=F32)
        factor = jnp.dot(
            grown, spread(heads, lanes, hsize, j * lanes), preferred_element_type=F32
        )
        y = y_ref[:, at] + factor * carried
        z = z_ref[:, at].astype(F32)
        value = y * (z / (1.0 + jnp.exp(-z)))
        gated[:, at] = value
        square = square + jnp.sum(value * value, axis=1, keepdims=True)
    scale = lax.rsqrt(square / width + 1e-05)
    for j in range(parts):
        at = slice(j * lanes, (j + 1) * lanes)
        out_ref[:, at] = (gated[:, at] * scale * gain_ref[:, at]).astype(BF)


def gated_norm(y, zs, cs, cum, state, gain, row_tile):
    rows, width = y.shape
    heads, nstate = cum.shape[1], cs.shape[1]
    return pl.pallas_call(
        functools.partial(norm_kernel, width // heads),
        grid=(rows // row_tile,),
        in_specs=[
            pl.BlockSpec((row_tile, width), lambda i: (i, 0)),
            pl.BlockSpec((row_tile, width), lambda i: (i, 0)),
            pl.BlockSpec((row_tile, nstate), lambda i: (i, 0)),
            pl.BlockSpec((row_tile, heads), lambda i: (i, 0)),
            pl.BlockSpec(state.shape, lambda i: (0, 0, 0)),
            pl.BlockSpec((1, width), lambda i: (0, 0)),
        ],
        out_specs=pl.BlockSpec((row_tile, width), lambda i: (i, 0)),
        out_shape=jax.ShapeDtypeStruct((rows, width), BF),
        scratch_shapes=[pltpu.VMEM((row_tile, width), F32)],
        cost_estimate=pl.CostEstimate(
            flops=2 * rows * width * nstate,
            bytes_accessed=16 * rows * width,
            transcendentals=rows * width,
        ),
        compiler_params=params(),
        name="gated_norm",
    )(y, zs, cs, cum, state, gain)


def per_device(
    tokens_x, gate_z, in_b, in_c, log_decay, domain_ids, out_weight, norm_gain, skip_gain
):
    groups = lax.axis_size("dom")
    seq = lax.axis_size("seq")
    me = lax.axis_index("seq")
    rows, width = tokens_x.shape
    nstate = in_b.shape[1]
    heads = log_decay.shape[1]
    hsize = width // heads
    columns = out_weight.shape[2]

    bits = [1 << i for i in range(seq.bit_length() - 1) if 1 << i != PARTNER]
    bits = bits[1:][::-1] + bits[:1]
    pieces = {0: out_weight[0]}
    for bit in bits:
        pieces.update({k | bit: exchange(piece, "seq", bit) for k, piece in list(pieces.items())})

    ids = domain_ids.reshape(1, groups)
    order = jnp.sum(
        jnp.where(
            ids == jnp.arange(groups, dtype=jnp.int32)[:, None],
            jnp.arange(groups, dtype=jnp.int32)[None, :],
            0,
        ),
        axis=1,
    ).astype(jnp.int32)
    pad = jnp.zeros((rows, 128 - heads), log_decay.dtype) if heads < 128 else log_decay[:, :0]
    small = jnp.concatenate([in_b, in_c, log_decay, pad], axis=1)
    x_out, z_out, small_out = arrange(order, (tokens_x, gate_z, small), groups)
    send = functools.partial(
        lax.all_to_all, axis_name="dom", split_axis=0, concat_axis=0, tiled=True
    )
    small_in = send(small_out)
    xs = send(x_out)
    zs = send(z_out)
    bs = small_in[:, :nstate]
    cs = small_in[:, nstate : 2 * nstate]
    ls = small_in[:, 2 * nstate : 2 * nstate + heads]

    ends, cum = block_states(xs, bs, ls, seq)
    totals = jnp.broadcast_to(cum[-1].reshape(seq, heads // seq, 1), (seq, heads // seq, hsize))
    totals = totals.reshape(seq, 1, width // seq)
    over = functools.partial(
        lax.all_to_all, axis_name="seq", split_axis=0, concat_axis=0, tiled=True
    )
    totals = over(totals).reshape(seq, width // seq)
    before = over(prefix_states(over(ends), totals))

    skip = jnp.repeat(skip_gain, hsize, axis=1)
    y = inner_part(xs, bs, cs, cum, skip)
    normed = gated_norm(y, zs, cs, cum, before, norm_gain, 64)

    theirs = exchange(normed, "seq", PARTNER)

    def project(acts, piece):
        return jnp.dot(acts, piece, preferred_element_type=F32).astype(BF)

    keys = sorted(pieces)
    outward = jnp.concatenate([project(theirs, pieces[k]) for k in keys], axis=1)
    inward = exchange(outward, "seq", PARTNER)
    out = jnp.zeros((rows, seq * columns), BF)
    for i, k in enumerate(keys):
        out = lax.dynamic_update_slice(out, project(normed, pieces[k]), (0, (me ^ k) * columns))
    for i, k in enumerate(keys):
        block = inward[:, i * columns : (i + 1) * columns]
        out = lax.dynamic_update_slice(out, block, (0, (me ^ (k | PARTNER)) * columns))
    return out[None]


def solution(mesh):
    in_specs = (
        P(("dom", "seq"), None),
        P(("dom", "seq"), None),
        P(("dom", "seq"), None),
        P(("dom", "seq"), None),
        P(("dom", "seq"), None),
        P("dom", "seq", None),
        P("dom", None, "seq"),
        P("dom", None),
        P("dom", None),
    )
    return jax.shard_map(
        per_device, mesh=mesh, in_specs=in_specs, out_specs=P("dom", "seq", None), check_vma=False
    )
```

```python
import functools

import jax
import jax.numpy as jnp
from jax import lax
from jax.experimental import pallas as pl
from jax.experimental.pallas import tpu as pltpu
from jax.sharding import PartitionSpec as P

BF = jnp.bfloat16
F32 = jnp.float32
PARTNER = 2


def params(**extra):
    return pltpu.CompilerParams(vmem_limit_bytes=48 * 1024 * 1024, **extra)


def exchange(block, axis, bit):
    size = lax.axis_size(axis)
    return lax.ppermute(block, axis, [(i, i ^ bit) for i in range(size)])


def join_block(order_ref, x_ref, z_ref, small_ref, out_ref):
    width = x_ref.shape[1]
    out_ref[:, :width] = x_ref[...]
    out_ref[:, width : 2 * width] = z_ref[...]
    out_ref[:, 2 * width :] = small_ref[...]


def arrange(order, arrays, groups):
    rows = arrays[0].shape[0]
    seg = rows // groups
    total = sum(a.shape[1] for a in arrays)
    return pl.pallas_call(
        join_block,
        grid_spec=pltpu.PrefetchScalarGridSpec(
            num_scalar_prefetch=1,
            grid=(groups,),
            in_specs=[
                pl.BlockSpec((seg, a.shape[1]), lambda d, o: (o[d], 0)) for a in arrays
            ],
            out_specs=pl.BlockSpec((seg, total), lambda d, o: (d, 0)),
        ),
        out_shape=jax.ShapeDtypeStruct((rows, total), BF),
        compiler_params=params(),
        name="arrange",
    )(order, *arrays)


def split2(value):
    high = value.astype(BF)
    low = (value - high.astype(F32)).astype(BF)
    return jnp.concatenate([high, low], axis=1)


def spread(heads, lanes, hsize, start):
    row = lax.broadcasted_iota(jnp.int32, (2 * heads, lanes), 0)
    lane = lax.broadcasted_iota(jnp.int32, (2 * heads, lanes), 1) + start
    row = jnp.where(row >= heads, row - heads, row)
    return jnp.where((lane >= row * hsize) & (lane < (row + 1) * hsize), 1.0, 0.0).astype(BF)


def state_kernel(hsize, heads, x_ref, b_ref, l_ref, state_ref, cum_ref, tail, bt, total):
    rows, lanes = x_ref.shape
    nstate = b_ref.shape[1]

    @pl.when(pl.program_id(0) == 0)
    def _():
        t = lax.broadcasted_iota(jnp.int32, (rows, rows), 0)
        u = lax.broadcasted_iota(jnp.int32, (rows, rows), 1)
        lower = jnp.where(t >= u, 1.0, 0.0).astype(BF)
        cum = jnp.dot(lower, l_ref[:, :heads], preferred_element_type=F32)
        cum_ref[...] = cum
        last = cum[rows - 1 : rows, :]
        tail[...] = split2(jnp.exp(last - cum))
        bt[...] = jnp.transpose(b_ref[...].astype(F32)).astype(BF)
        first = last.astype(BF).astype(F32)
        second = (last - first).astype(BF).astype(F32)
        third = last - first - second
        row = lax.broadcasted_iota(jnp.int32, total.shape, 0)
        total[...] = jnp.where(
            row == 0, first, jnp.where(row == 1, second, jnp.where(row == 2, third, 0.0))
        ).astype(BF)

    choose = spread(heads, lanes, hsize, pl.program_id(0) * lanes)
    factor = jnp.dot(tail[...], choose, preferred_element_type=F32)
    decayed = (x_ref[...].astype(F32) * factor).astype(BF)
    state_ref[0, :nstate] = jnp.dot(bt[...], decayed, preferred_element_type=F32).astype(BF)
    state_ref[0, nstate:] = jnp.dot(
        total[...], choose[:heads], preferred_element_type=F32
    ).astype(BF)


def block_states(joined, width, heads, nstate, parts):
    rows = joined.shape[0]
    lanes = width // parts
    at = 2 * width // nstate
    return pl.pallas_call(
        functools.partial(state_kernel, width // heads, heads),
        grid=(parts,),
        in_specs=[
            pl.BlockSpec((rows, lanes), lambda j: (0, j)),
            pl.BlockSpec((rows, nstate), lambda j: (0, at)),
            pl.BlockSpec((rows, nstate), lambda j: (0, at + 2)),
        ],
        out_specs=[
            pl.BlockSpec((1, nstate + 16, lanes), lambda j: (j, 0, 0)),
            pl.BlockSpec((rows, heads), lambda j: (0, 0)),
        ],
        out_shape=[
            jax.ShapeDtypeStruct((parts, nstate + 16, lanes), BF),
            jax.ShapeDtypeStruct((rows, heads), F32),
        ],
        scratch_shapes=[
            pltpu.VMEM((rows, 2 * heads), BF),
            pltpu.VMEM((nstate, rows), BF),
            pltpu.VMEM((16, heads), BF),
        ],
        cost_estimate=pl.CostEstimate(
            flops=2 * rows * width * nstate, bytes_accessed=4 * rows * width, transcendentals=0
        ),
        compiler_params=params(),
        name="block_states",
    )(joined, joined, joined)


def inner_kernel(hsize, x_ref, b_ref, c_ref, cum_ref, cumt_ref, skip_ref, y_ref, scores):
    rows = x_ref.shape[0]
    group = cumt_ref.shape[1]
    half = rows // 2

    @pl.when(pl.program_id(0) == 0)
    def _():
        scores[...] = lax.dot_general(
            c_ref[...], b_ref[...], (((1,), (1,)), ((), ())), preferred_element_type=F32
        )

    lane = lax.broadcasted_iota(jnp.int32, (half, 2 * hsize), 1)

    def product(part, h, x_pair):
        top = part * half
        cols = top + half
        t = lax.broadcasted_iota(jnp.int32, (half, cols), 0) + top
        u = lax.broadcasted_iota(jnp.int32, (half, cols), 1)
        diff = cum_ref[0, top : top + half, h : h + 1] - cumt_ref[0, h : h + 1, :cols]
        decay = jnp.where(t >= u, jnp.exp(jnp.minimum(diff, 0.0)), 0.0)
        weights = (scores[top : top + half, :cols] * decay).astype(BF)
        return jnp.dot(weights, x_pair[:cols], preferred_element_type=F32)

    for pair in range(group // 2):
        at = slice(pair * 2 * hsize, (pair + 1) * 2 * hsize)
        x_pair = x_ref[:, at]
        for part in range(2):
            span = slice(part * half, (part + 1) * half)
            first = product(part, 2 * pair, x_pair)
            second = product(part, 2 * pair + 1, x_pair)
            y_ref[span, at] = (
                jnp.where(lane < hsize, first, second)
                + skip_ref[:, at] * x_pair[span].astype(F32)
            )


def inner_part(joined, nstate, cum, skip):
    width = skip.shape[1]
    rows, heads = cum.shape
    at = 2 * width // nstate
    steps = heads // 8
    lanes = width // steps
    cum_groups = jnp.transpose(cum.reshape(rows, steps, 8), (1, 0, 2))
    cumt = jnp.transpose(cum_groups, (0, 2, 1))
    return pl.pallas_call(
        functools.partial(inner_kernel, width // heads),
        grid=(steps,),
        in_specs=[
            pl.BlockSpec((rows, lanes), lambda j: (0, j)),
            pl.BlockSpec((rows, nstate), lambda j: (0, at)),
            pl.BlockSpec((rows, nstate), lambda j: (0, at + 1)),
            pl.BlockSpec((1, rows, 8), lambda j: (j, 0, 0)),
            pl.BlockSpec((1, 8, rows), lambda j: (j, 0, 0)),
            pl.BlockSpec((1, lanes), lambda j: (0, j)),
        ],
        out_specs=pl.BlockSpec((rows, lanes), lambda j: (0, j)),
        out_shape=jax.ShapeDtypeStruct((rows, width), F32),
        scratch_shapes=[pltpu.VMEM((rows, rows), F32)],
        cost_estimate=pl.CostEstimate(
            flops=16 * rows * rows * width // 4,
            bytes_accessed=40 * rows * width,
            transcendentals=heads * rows * rows,
        ),
        compiler_params=params(),
        name="inner_part",
    )(joined, joined, joined, cum_groups, cumt, skip)


def prefix_kernel(end_ref, before_ref):
    parts, nstate, _ = before_ref.shape
    running = jnp.zeros(before_ref.shape[1:], F32)
    for s in range(parts):
        before_ref[s] = running.astype(BF)
        if s < parts - 1:
            terms = end_ref[s, nstate:].astype(F32)
            total = jnp.sum(terms, axis=0, keepdims=True)
            running = jnp.exp(total) * running + end_ref[s, :nstate].astype(F32)


def prefix_states(ends):
    parts, tall, lanes = ends.shape
    vmem = pl.BlockSpec(memory_space=pltpu.VMEM)
    return pl.pallas_call(
        prefix_kernel,
        in_specs=[vmem],
        out_specs=vmem,
        out_shape=jax.ShapeDtypeStruct((parts, tall - 16, lanes), BF),
        compiler_params=params(),
        name="prefix_states",
    )(ends)


def norm_kernel(hsize, y_ref, z_ref, c_ref, cum_ref, state_ref, gain_ref, out_ref, gated):
    rows, width = y_ref.shape
    heads = cum_ref.shape[1]
    parts, _, lanes = state_ref.shape
    grown = split2(jnp.exp(cum_ref[...]))
    square = jnp.zeros((rows, 1), F32)
    for j in range(parts):
        at = slice(j * lanes, (j + 1) * lanes)
        carried = jnp.dot(c_ref[...], state_ref[j], preferred_element_type=F32)
        factor = jnp.dot(
            grown, spread(heads, lanes, hsize, j * lanes), preferred_element_type=F32
        )
        y = y_ref[:, at] + factor * carried
        z = z_ref[:, at].astype(F32)
        value = y * (z / (1.0 + jnp.exp(-z)))
        gated[:, at] = value
        square = square + jnp.sum(value * value, axis=1, keepdims=True)
    scale = lax.rsqrt(square / width + 1e-05)
    for j in range(parts):
        at = slice(j * lanes, (j + 1) * lanes)
        out_ref[:, at] = (gated[:, at] * scale * gain_ref[:, at]).astype(BF)


def gated_norm(y, joined, cum, state, gain, row_tile):
    rows, width = y.shape
    heads, nstate = cum.shape[1], state.shape[1]
    at = 2 * width // nstate
    return pl.pallas_call(
        functools.partial(norm_kernel, width // heads),
        grid=(rows // row_tile,),
        in_specs=[
            pl.BlockSpec((row_tile, width), lambda i: (i, 0)),
            pl.BlockSpec((row_tile, width), lambda i: (i, 1)),
            pl.BlockSpec((row_tile, nstate), lambda i: (i, at + 1)),
            pl.BlockSpec((row_tile, heads), lambda i: (i, 0)),
            pl.BlockSpec(state.shape, lambda i: (0, 0, 0)),
            pl.BlockSpec((1, width), lambda i: (0, 0)),
        ],
        out_specs=pl.BlockSpec((row_tile, width), lambda i: (i, 0)),
        out_shape=jax.ShapeDtypeStruct((rows, width), BF),
        scratch_shapes=[pltpu.VMEM((row_tile, width), F32)],
        cost_estimate=pl.CostEstimate(
            flops=2 * rows * width * nstate,
            bytes_accessed=16 * rows * width,
            transcendentals=rows * width,
        ),
        compiler_params=params(),
        name="gated_norm",
    )(y, joined, joined, cum, state, gain)


def per_device(
    tokens_x, gate_z, in_b, in_c, log_decay, domain_ids, out_weight, norm_gain, skip_gain
):
    groups = lax.axis_size("dom")
    seq = lax.axis_size("seq")
    me = lax.axis_index("seq")
    rows, width = tokens_x.shape
    nstate = in_b.shape[1]
    heads = log_decay.shape[1]
    hsize = width // heads
    columns = out_weight.shape[2]

    ids = domain_ids.reshape(1, groups)
    order = jnp.sum(
        jnp.where(
            ids == jnp.arange(groups, dtype=jnp.int32)[:, None],
            jnp.arange(groups, dtype=jnp.int32)[None, :],
            0,
        ),
        axis=1,
    ).astype(jnp.int32)
    pad = jnp.zeros((rows, nstate - heads), log_decay.dtype)
    small = jnp.concatenate([in_b, in_c, log_decay, pad], axis=1)
    joined = lax.all_to_all(
        arrange(order, (tokens_x, gate_z, small), groups),
        "dom",
        split_axis=0,
        concat_axis=0,
        tiled=True,
    )

    unit = columns // 4
    bits = [1 << i for i in range(seq.bit_length() - 1)]
    far = [bit for bit in bits if bit not in (1, PARTNER)]
    own = out_weight[0]

    def cut(first, units):
        return own[:, first * unit : (first + units) * unit]

    def far_pieces(block):
        found = {0: block}
        for bit in far[::-1]:
            found.update({k | bit: exchange(v, "seq", bit) for k, v in list(found.items())})
        del found[0]
        return found

    def forward(found):
        return {k | 1: exchange(v, "seq", 1) for k, v in found.items()}

    done = []

    near_a = exchange(cut(0, 2), "seq", 1)
    far_a = far_pieces(cut(0, 1))
    joined, near_a, far_a = lax.optimization_barrier((joined, near_a, far_a))

    ends, cum = block_states(joined, width, heads, nstate, seq)
    over = functools.partial(
        lax.all_to_all, axis_name="seq", split_axis=0, concat_axis=0, tiled=True
    )
    before = over(prefix_states(over(ends)))
    skip = jnp.repeat(skip_gain, hsize, axis=1)
    y = inner_part(joined, nstate, cum, skip)

    before, far_a, own_b, own_c, own_d = lax.optimization_barrier(
        (before, far_a, cut(1, 2), cut(3, 1), cut(2, 2))
    )
    far_b = far_pieces(own_b)
    near_b = exchange(own_d, "seq", 1)
    forward_a = forward(far_a)
    forward_b = forward(far_b)
    own_c, far_b = lax.optimization_barrier((own_c, far_b))
    far_c = far_pieces(own_c)
    forward_c = forward(far_c)

    normed = gated_norm(y, joined, cum, before, norm_gain, 64)
    theirs = exchange(normed, "seq", PARTNER)
    acts = jnp.concatenate([normed, theirs], axis=0)

    early = [
        (0, {0: own}),
        (0, {1: near_a}),
        (0, far_a),
        (0, forward_a),
        (2, {1: near_b}),
        (1, far_b),
    ]
    late = [(1, forward_b), (3, far_c), (3, forward_c)]

    out = jnp.zeros((rows, seq * columns), BF)
    returned = []
    for batch in (early, late):
        places, blocks = [], []
        for first, found in batch:
            for key, piece in found.items():
                block = jnp.dot(acts, piece, preferred_element_type=F32).astype(BF)
                at = first * unit
                out = lax.dynamic_update_slice(out, block[:rows], (0, (me ^ key) * columns + at))
                places.append((key, at, piece.shape[1]))
                blocks.append(block[rows:])
        returned.append((places, exchange(jnp.concatenate(blocks, axis=1), "seq", PARTNER)))
    for places, block in returned:
        start = 0
        for key, at, wide in places:
            out = lax.dynamic_update_slice(
                out,
                block[:, start : start + wide],
                (0, (me ^ (key | PARTNER)) * columns + at),
            )
            start += wide
    return out[None]


def solution(mesh):
    in_specs = (
        P(("dom", "seq"), None),
        P(("dom", "seq"), None),
        P(("dom", "seq"), None),
        P(("dom", "seq"), None),
        P(("dom", "seq"), None),
        P("dom", "seq", None),
        P("dom", None, "seq"),
        P("dom", None),
        P("dom", None),
    )
    return jax.shard_map(
        per_device, mesh=mesh, in_specs=in_specs, out_specs=P("dom", "seq", None), check_vma=False
    )
```

```python
import functools

import jax
import jax.numpy as jnp
from jax import lax
from jax.experimental import pallas as pl
from jax.experimental.pallas import tpu as pltpu
from jax.sharding import PartitionSpec as P

BF = jnp.bfloat16
F32 = jnp.float32
PARTNER = 4


def params(**extra):
    return pltpu.CompilerParams(vmem_limit_bytes=48 * 1024 * 1024, **extra)


def exchange(block, axis, bit):
    size = lax.axis_size(axis)
    return lax.ppermute(block, axis, [(i, i ^ bit) for i in range(size)])


def join_block(order_ref, x_ref, z_ref, small_ref, out_ref):
    width = x_ref.shape[1]
    out_ref[:, :width] = x_ref[...]
    out_ref[:, width : 2 * width] = z_ref[...]
    out_ref[:, 2 * width :] = small_ref[...]


def arrange(order, arrays, groups):
    rows = arrays[0].shape[0]
    seg = rows // groups
    total = sum(a.shape[1] for a in arrays)
    return pl.pallas_call(
        join_block,
        grid_spec=pltpu.PrefetchScalarGridSpec(
            num_scalar_prefetch=1,
            grid=(groups,),
            in_specs=[
                pl.BlockSpec((seg, a.shape[1]), lambda d, o: (o[d], 0)) for a in arrays
            ],
            out_specs=pl.BlockSpec((seg, total), lambda d, o: (d, 0)),
        ),
        out_shape=jax.ShapeDtypeStruct((rows, total), BF),
        compiler_params=params(),
        name="arrange",
    )(order, *arrays)


def split2(value):
    high = value.astype(BF)
    low = (value - high.astype(F32)).astype(BF)
    return jnp.concatenate([high, low], axis=1)


def spread(heads, lanes, hsize, start):
    row = lax.broadcasted_iota(jnp.int32, (2 * heads, lanes), 0)
    lane = lax.broadcasted_iota(jnp.int32, (2 * heads, lanes), 1) + start
    row = jnp.where(row >= heads, row - heads, row)
    return jnp.where((lane >= row * hsize) & (lane < (row + 1) * hsize), 1.0, 0.0).astype(BF)


def state_kernel(hsize, heads, x_ref, b_ref, l_ref, state_ref, cum_ref, tail, bt, total):
    rows, lanes = x_ref.shape
    nstate = b_ref.shape[1]

    @pl.when(pl.program_id(0) == 0)
    def _():
        t = lax.broadcasted_iota(jnp.int32, (rows, rows), 0)
        u = lax.broadcasted_iota(jnp.int32, (rows, rows), 1)
        lower = jnp.where(t >= u, 1.0, 0.0).astype(BF)
        cum = jnp.dot(lower, l_ref[:, :heads], preferred_element_type=F32)
        cum_ref[...] = cum
        last = cum[rows - 1 : rows, :]
        tail[...] = split2(jnp.exp(last - cum))
        bt[...] = jnp.transpose(b_ref[...].astype(F32)).astype(BF)
        first = last.astype(BF).astype(F32)
        second = (last - first).astype(BF).astype(F32)
        third = last - first - second
        row = lax.broadcasted_iota(jnp.int32, total.shape, 0)
        total[...] = jnp.where(
            row == 0, first, jnp.where(row == 1, second, jnp.where(row == 2, third, 0.0))
        ).astype(BF)

    choose = spread(heads, lanes, hsize, pl.program_id(0) * lanes)
    factor = jnp.dot(tail[...], choose, preferred_element_type=F32)
    decayed = (x_ref[...].astype(F32) * factor).astype(BF)
    state_ref[0, :nstate] = jnp.dot(bt[...], decayed, preferred_element_type=F32).astype(BF)
    state_ref[0, nstate:] = jnp.dot(
        total[...], choose[:heads], preferred_element_type=F32
    ).astype(BF)


def block_states(joined, width, heads, nstate, parts):
    rows = joined.shape[0]
    lanes = width // parts
    at = 2 * width // nstate
    return pl.pallas_call(
        functools.partial(state_kernel, width // heads, heads),
        grid=(parts,),
        in_specs=[
            pl.BlockSpec((rows, lanes), lambda j: (0, j)),
            pl.BlockSpec((rows, nstate), lambda j: (0, at)),
            pl.BlockSpec((rows, nstate), lambda j: (0, at + 2)),
        ],
        out_specs=[
            pl.BlockSpec((1, nstate + 16, lanes), lambda j: (j, 0, 0)),
            pl.BlockSpec((rows, heads), lambda j: (0, 0)),
        ],
        out_shape=[
            jax.ShapeDtypeStruct((parts, nstate + 16, lanes), BF),
            jax.ShapeDtypeStruct((rows, heads), F32),
        ],
        scratch_shapes=[
            pltpu.VMEM((rows, 2 * heads), BF),
            pltpu.VMEM((nstate, rows), BF),
            pltpu.VMEM((16, heads), BF),
        ],
        cost_estimate=pl.CostEstimate(
            flops=2 * rows * width * nstate, bytes_accessed=4 * rows * width, transcendentals=0
        ),
        compiler_params=params(),
        name="block_states",
    )(joined, joined, joined)


def inner_kernel(hsize, x_ref, b_ref, c_ref, cum_ref, cumt_ref, skip_ref, y_ref, scores):
    rows = x_ref.shape[0]
    group = cumt_ref.shape[1]
    half = rows // 2

    @pl.when(pl.program_id(0) == 0)
    def _():
        scores[...] = lax.dot_general(
            c_ref[...], b_ref[...], (((1,), (1,)), ((), ())), preferred_element_type=F32
        )

    lane = lax.broadcasted_iota(jnp.int32, (half, 2 * hsize), 1)

    def product(part, h, x_pair):
        top = part * half
        cols = top + half
        t = lax.broadcasted_iota(jnp.int32, (half, cols), 0) + top
        u = lax.broadcasted_iota(jnp.int32, (half, cols), 1)
        diff = cum_ref[0, top : top + half, h : h + 1] - cumt_ref[0, h : h + 1, :cols]
        decay = jnp.where(t >= u, jnp.exp(jnp.minimum(diff, 0.0)), 0.0)
        weights = (scores[top : top + half, :cols] * decay).astype(BF)
        return jnp.dot(weights, x_pair[:cols], preferred_element_type=F32)

    for pair in range(group // 2):
        at = slice(pair * 2 * hsize, (pair + 1) * 2 * hsize)
        x_pair = x_ref[:, at]
        for part in range(2):
            span = slice(part * half, (part + 1) * half)
            first = product(part, 2 * pair, x_pair)
            second = product(part, 2 * pair + 1, x_pair)
            y_ref[span, at] = (
                jnp.where(lane < hsize, first, second)
                + skip_ref[:, at] * x_pair[span].astype(F32)
            )


def inner_part(joined, nstate, cum, skip):
    width = skip.shape[1]
    rows, heads = cum.shape
    at = 2 * width // nstate
    steps = heads // 8
    lanes = width // steps
    cum_groups = jnp.transpose(cum.reshape(rows, steps, 8), (1, 0, 2))
    cumt = jnp.transpose(cum_groups, (0, 2, 1))
    return pl.pallas_call(
        functools.partial(inner_kernel, width // heads),
        grid=(steps,),
        in_specs=[
            pl.BlockSpec((rows, lanes), lambda j: (0, j)),
            pl.BlockSpec((rows, nstate), lambda j: (0, at)),
            pl.BlockSpec((rows, nstate), lambda j: (0, at + 1)),
            pl.BlockSpec((1, rows, 8), lambda j: (j, 0, 0)),
            pl.BlockSpec((1, 8, rows), lambda j: (j, 0, 0)),
            pl.BlockSpec((1, lanes), lambda j: (0, j)),
        ],
        out_specs=pl.BlockSpec((rows, lanes), lambda j: (0, j)),
        out_shape=jax.ShapeDtypeStruct((rows, width), F32),
        scratch_shapes=[pltpu.VMEM((rows, rows), F32)],
        cost_estimate=pl.CostEstimate(
            flops=16 * rows * rows * width // 4,
            bytes_accessed=40 * rows * width,
            transcendentals=heads * rows * rows,
        ),
        compiler_params=params(),
        name="inner_part",
    )(joined, joined, joined, cum_groups, cumt, skip)


def prefix_kernel(end_ref, before_ref):
    parts, nstate, _ = before_ref.shape
    running = jnp.zeros(before_ref.shape[1:], F32)
    for s in range(parts):
        before_ref[s] = running.astype(BF)
        if s < parts - 1:
            terms = end_ref[s, nstate:].astype(F32)
            total = jnp.sum(terms, axis=0, keepdims=True)
            running = jnp.exp(total) * running + end_ref[s, :nstate].astype(F32)


def prefix_states(ends):
    parts, tall, lanes = ends.shape
    vmem = pl.BlockSpec(memory_space=pltpu.VMEM)
    return pl.pallas_call(
        prefix_kernel,
        in_specs=[vmem],
        out_specs=vmem,
        out_shape=jax.ShapeDtypeStruct((parts, tall - 16, lanes), BF),
        compiler_params=params(),
        name="prefix_states",
    )(ends)


def norm_kernel(hsize, y_ref, z_ref, c_ref, cum_ref, state_ref, gain_ref, out_ref, gated):
    rows, width = y_ref.shape
    heads = cum_ref.shape[1]
    parts, _, lanes = state_ref.shape
    grown = split2(jnp.exp(cum_ref[...]))
    square = jnp.zeros((rows, 1), F32)
    for j in range(parts):
        at = slice(j * lanes, (j + 1) * lanes)
        carried = jnp.dot(c_ref[...], state_ref[j], preferred_element_type=F32)
        factor = jnp.dot(
            grown, spread(heads, lanes, hsize, j * lanes), preferred_element_type=F32
        )
        y = y_ref[:, at] + factor * carried
        z = z_ref[:, at].astype(F32)
        value = y * (z / (1.0 + jnp.exp(-z)))
        gated[:, at] = value
        square = square + jnp.sum(value * value, axis=1, keepdims=True)
    scale = lax.rsqrt(square / width + 1e-05)
    for j in range(parts):
        at = slice(j * lanes, (j + 1) * lanes)
        out_ref[:, at] = (gated[:, at] * scale * gain_ref[:, at]).astype(BF)


def gated_norm(y, joined, cum, state, gain, row_tile):
    rows, width = y.shape
    heads, nstate = cum.shape[1], state.shape[1]
    at = 2 * width // nstate
    return pl.pallas_call(
        functools.partial(norm_kernel, width // heads),
        grid=(rows // row_tile,),
        in_specs=[
            pl.BlockSpec((row_tile, width), lambda i: (i, 0)),
            pl.BlockSpec((row_tile, width), lambda i: (i, 1)),
            pl.BlockSpec((row_tile, nstate), lambda i: (i, at + 1)),
            pl.BlockSpec((row_tile, heads), lambda i: (i, 0)),
            pl.BlockSpec(state.shape, lambda i: (0, 0, 0)),
            pl.BlockSpec((1, width), lambda i: (0, 0)),
        ],
        out_specs=pl.BlockSpec((row_tile, width), lambda i: (i, 0)),
        out_shape=jax.ShapeDtypeStruct((rows, width), BF),
        scratch_shapes=[pltpu.VMEM((row_tile, width), F32)],
        cost_estimate=pl.CostEstimate(
            flops=2 * rows * width * nstate,
            bytes_accessed=16 * rows * width,
            transcendentals=rows * width,
        ),
        compiler_params=params(),
        name="gated_norm",
    )(y, joined, joined, cum, state, gain)


def per_device(
    tokens_x, gate_z, in_b, in_c, log_decay, domain_ids, out_weight, norm_gain, skip_gain
):
    groups = lax.axis_size("dom")
    seq = lax.axis_size("seq")
    me = lax.axis_index("seq")
    rows, width = tokens_x.shape
    nstate = in_b.shape[1]
    heads = log_decay.shape[1]
    hsize = width // heads
    columns = out_weight.shape[2]

    ids = domain_ids.reshape(1, groups)
    order = jnp.sum(
        jnp.where(
            ids == jnp.arange(groups, dtype=jnp.int32)[:, None],
            jnp.arange(groups, dtype=jnp.int32)[None, :],
            0,
        ),
        axis=1,
    ).astype(jnp.int32)
    pad = jnp.zeros((rows, nstate - heads), log_decay.dtype)
    small = jnp.concatenate([in_b, in_c, log_decay, pad], axis=1)
    joined = lax.all_to_all(
        arrange(order, (tokens_x, gate_z, small), groups),
        "dom",
        split_axis=0,
        concat_axis=0,
        tiled=True,
    )

    half = columns // 2
    bits = [1 << i for i in range(seq.bit_length() - 1)]
    far = [bit for bit in bits if bit not in (1, PARTNER)]

    def far_pieces(block):
        found = {0: block}
        for bit in far:
            found.update({k | bit: exchange(v, "seq", bit) for k, v in list(found.items())})
        del found[0]
        return found

    def forward(found):
        return {k | 1: exchange(v, "seq", 1) for k, v in found.items()}

    own_a, own_b = out_weight[0, :, :half], out_weight[0, :, half:]
    far_a = far_pieces(own_a)
    near_a = exchange(own_a, "seq", 1)
    joined, near_a, far_a = lax.optimization_barrier((joined, near_a, far_a))
    forward_a = forward(far_a)

    ends, cum = block_states(joined, width, heads, nstate, seq)
    over = functools.partial(
        lax.all_to_all, axis_name="seq", split_axis=0, concat_axis=0, tiled=True
    )
    prefix = prefix_states(over(ends))
    prefix, far_own, forward_a = lax.optimization_barrier((prefix, own_b, forward_a))
    far_b = far_pieces(far_own)
    before = over(prefix)
    skip = jnp.repeat(skip_gain, hsize, axis=1)
    y = inner_part(joined, nstate, cum, skip)

    before, near_own = lax.optimization_barrier((before, own_b))
    near_b = exchange(near_own, "seq", 1)
    forward_b = forward(far_b)

    normed = gated_norm(y, joined, cum, before, norm_gain, 64)
    theirs = exchange(normed, "seq", PARTNER)

    early = [(0, {0: own_a, 1: near_a}), (half, {0: own_b}), (0, far_a), (0, forward_a)]
    late = [(half, {1: near_b}), (half, far_b)]
    last = [(half, forward_b)]

    def project(acts, piece):
        return jnp.dot(acts, piece, preferred_element_type=F32).astype(BF)

    out = jnp.zeros((rows, seq * columns), BF)
    returned = []
    for batch in (early, late, last):
        places, blocks = [], []
        for at, found in batch:
            for key, piece in found.items():
                out = lax.dynamic_update_slice(
                    out, project(normed, piece), (0, (me ^ key) * columns + at)
                )
                places.append((key, at))
                blocks.append(project(theirs, piece))
        returned.append((places, exchange(jnp.stack(blocks), "seq", PARTNER)))
    for places, block in returned:
        for i, (key, at) in enumerate(places):
            out = lax.dynamic_update_slice(
                out, block[i], (0, (me ^ (key | PARTNER)) * columns + at)
            )
    return out[None]


def solution(mesh):
    in_specs = (
        P(("dom", "seq"), None),
        P(("dom", "seq"), None),
        P(("dom", "seq"), None),
        P(("dom", "seq"), None),
        P(("dom", "seq"), None),
        P("dom", "seq", None),
        P("dom", None, "seq"),
        P("dom", None),
        P("dom", None),
    )
    return jax.shard_map(
        per_device, mesh=mesh, in_specs=in_specs, out_specs=P("dom", "seq", None), check_vma=False
    )
```

```python
import functools

import jax
import jax.numpy as jnp
from jax import lax
from jax.experimental import pallas as pl
from jax.experimental.pallas import tpu as pltpu
from jax.sharding import PartitionSpec as P

BF = jnp.bfloat16
F32 = jnp.float32
PARTNER = 4


def params(**extra):
    return pltpu.CompilerParams(vmem_limit_bytes=48 * 1024 * 1024, **extra)


def exchange(block, axis, bit):
    size = lax.axis_size(axis)
    return lax.ppermute(block, axis, [(i, i ^ bit) for i in range(size)])


def join_block(order_ref, x_ref, z_ref, small_ref, out_ref):
    width = x_ref.shape[1]
    out_ref[:, :width] = x_ref[...]
    out_ref[:, width : 2 * width] = z_ref[...]
    out_ref[:, 2 * width :] = small_ref[...]


def arrange(order, arrays, groups):
    rows = arrays[0].shape[0]
    seg = rows // groups
    total = sum(a.shape[1] for a in arrays)
    return pl.pallas_call(
        join_block,
        grid_spec=pltpu.PrefetchScalarGridSpec(
            num_scalar_prefetch=1,
            grid=(groups,),
            in_specs=[
                pl.BlockSpec((seg, a.shape[1]), lambda d, o: (o[d], 0)) for a in arrays
            ],
            out_specs=pl.BlockSpec((seg, total), lambda d, o: (d, 0)),
        ),
        out_shape=jax.ShapeDtypeStruct((rows, total), BF),
        compiler_params=params(),
        name="arrange",
    )(order, *arrays)


def split2(value):
    high = value.astype(BF)
    low = (value - high.astype(F32)).astype(BF)
    return jnp.concatenate([high, low], axis=1)


def spread(heads, lanes, hsize, start):
    row = lax.broadcasted_iota(jnp.int32, (2 * heads, lanes), 0)
    lane = lax.broadcasted_iota(jnp.int32, (2 * heads, lanes), 1) + start
    row = jnp.where(row >= heads, row - heads, row)
    return jnp.where((lane >= row * hsize) & (lane < (row + 1) * hsize), 1.0, 0.0).astype(BF)


def state_kernel(hsize, heads, x_ref, b_ref, l_ref, state_ref, cum_ref, tail, bt, total):
    rows, lanes = x_ref.shape
    nstate = b_ref.shape[1]

    @pl.when(pl.program_id(0) == 0)
    def _():
        t = lax.broadcasted_iota(jnp.int32, (rows, rows), 0)
        u = lax.broadcasted_iota(jnp.int32, (rows, rows), 1)
        lower = jnp.where(t >= u, 1.0, 0.0).astype(BF)
        cum = jnp.dot(lower, l_ref[:, :heads], preferred_element_type=F32)
        cum_ref[...] = cum
        last = cum[rows - 1 : rows, :]
        tail[...] = split2(jnp.exp(last - cum))
        bt[...] = jnp.transpose(b_ref[...].astype(F32)).astype(BF)
        first = last.astype(BF).astype(F32)
        second = (last - first).astype(BF).astype(F32)
        third = last - first - second
        row = lax.broadcasted_iota(jnp.int32, total.shape, 0)
        total[...] = jnp.where(
            row == 0, first, jnp.where(row == 1, second, jnp.where(row == 2, third, 0.0))
        ).astype(BF)

    choose = spread(heads, lanes, hsize, pl.program_id(0) * lanes)
    factor = jnp.dot(tail[...], choose, preferred_element_type=F32)
    decayed = (x_ref[...].astype(F32) * factor).astype(BF)
    state_ref[0, :nstate] = jnp.dot(bt[...], decayed, preferred_element_type=F32).astype(BF)
    state_ref[0, nstate:] = jnp.dot(
        total[...], choose[:heads], preferred_element_type=F32
    ).astype(BF)


def block_states(joined, width, heads, nstate, parts):
    rows = joined.shape[0]
    lanes = width // parts
    at = 2 * width // nstate
    return pl.pallas_call(
        functools.partial(state_kernel, width // heads, heads),
        grid=(parts,),
        in_specs=[
            pl.BlockSpec((rows, lanes), lambda j: (0, j)),
            pl.BlockSpec((rows, nstate), lambda j: (0, at)),
            pl.BlockSpec((rows, nstate), lambda j: (0, at + 2)),
        ],
        out_specs=[
            pl.BlockSpec((1, nstate + 16, lanes), lambda j: (j, 0, 0)),
            pl.BlockSpec((rows, heads), lambda j: (0, 0)),
        ],
        out_shape=[
            jax.ShapeDtypeStruct((parts, nstate + 16, lanes), BF),
            jax.ShapeDtypeStruct((rows, heads), F32),
        ],
        scratch_shapes=[
            pltpu.VMEM((rows, 2 * heads), BF),
            pltpu.VMEM((nstate, rows), BF),
            pltpu.VMEM((16, heads), BF),
        ],
        cost_estimate=pl.CostEstimate(
            flops=2 * rows * width * nstate, bytes_accessed=4 * rows * width, transcendentals=0
        ),
        compiler_params=params(),
        name="block_states",
    )(joined, joined, joined)


def inner_kernel(hsize, x_ref, b_ref, c_ref, cum_ref, cumt_ref, skip_ref, y_ref, scores):
    rows = x_ref.shape[0]
    group = cumt_ref.shape[1]
    half = rows // 2

    @pl.when(pl.program_id(0) == 0)
    def _():
        scores[...] = lax.dot_general(
            c_ref[...], b_ref[...], (((1,), (1,)), ((), ())), preferred_element_type=F32
        )

    lane = lax.broadcasted_iota(jnp.int32, (half, 2 * hsize), 1)

    def product(part, h, x_pair):
        top = part * half
        cols = top + half
        t = lax.broadcasted_iota(jnp.int32, (half, cols), 0) + top
        u = lax.broadcasted_iota(jnp.int32, (half, cols), 1)
        diff = cum_ref[0, top : top + half, h : h + 1] - cumt_ref[0, h : h + 1, :cols]
        decay = jnp.where(t >= u, jnp.exp(jnp.minimum(diff, 0.0)), 0.0)
        weights = (scores[top : top + half, :cols] * decay).astype(BF)
        return jnp.dot(weights, x_pair[:cols], preferred_element_type=F32)

    for pair in range(group // 2):
        at = slice(pair * 2 * hsize, (pair + 1) * 2 * hsize)
        x_pair = x_ref[:, at]
        for part in range(2):
            span = slice(part * half, (part + 1) * half)
            first = product(part, 2 * pair, x_pair)
            second = product(part, 2 * pair + 1, x_pair)
            y_ref[span, at] = (
                jnp.where(lane < hsize, first, second)
                + skip_ref[:, at] * x_pair[span].astype(F32)
            )


def inner_part(joined, nstate, cum, skip):
    width = skip.shape[1]
    rows, heads = cum.shape
    at = 2 * width // nstate
    steps = heads // 8
    lanes = width // steps
    cum_groups = jnp.transpose(cum.reshape(rows, steps, 8), (1, 0, 2))
    cumt = jnp.transpose(cum_groups, (0, 2, 1))
    return pl.pallas_call(
        functools.partial(inner_kernel, width // heads),
        grid=(steps,),
        in_specs=[
            pl.BlockSpec((rows, lanes), lambda j: (0, j)),
            pl.BlockSpec((rows, nstate), lambda j: (0, at)),
            pl.BlockSpec((rows, nstate), lambda j: (0, at + 1)),
            pl.BlockSpec((1, rows, 8), lambda j: (j, 0, 0)),
            pl.BlockSpec((1, 8, rows), lambda j: (j, 0, 0)),
            pl.BlockSpec((1, lanes), lambda j: (0, j)),
        ],
        out_specs=pl.BlockSpec((rows, lanes), lambda j: (0, j)),
        out_shape=jax.ShapeDtypeStruct((rows, width), F32),
        scratch_shapes=[pltpu.VMEM((rows, rows), F32)],
        cost_estimate=pl.CostEstimate(
            flops=16 * rows * rows * width // 4,
            bytes_accessed=40 * rows * width,
            transcendentals=heads * rows * rows,
        ),
        compiler_params=params(),
        name="inner_part",
    )(joined, joined, joined, cum_groups, cumt, skip)


def prefix_kernel(end_ref, before_ref):
    parts, nstate, _ = before_ref.shape
    running = jnp.zeros(before_ref.shape[1:], F32)
    for s in range(parts):
        before_ref[s] = running.astype(BF)
        if s < parts - 1:
            terms = end_ref[s, nstate:].astype(F32)
            total = jnp.sum(terms, axis=0, keepdims=True)
            running = jnp.exp(total) * running + end_ref[s, :nstate].astype(F32)


def prefix_states(ends):
    parts, tall, lanes = ends.shape
    vmem = pl.BlockSpec(memory_space=pltpu.VMEM)
    return pl.pallas_call(
        prefix_kernel,
        in_specs=[vmem],
        out_specs=vmem,
        out_shape=jax.ShapeDtypeStruct((parts, tall - 16, lanes), BF),
        compiler_params=params(),
        name="prefix_states",
    )(ends)


def norm_kernel(hsize, y_ref, z_ref, c_ref, cum_ref, state_ref, gain_ref, out_ref, gated):
    rows, width = y_ref.shape
    heads = cum_ref.shape[1]
    parts, _, lanes = state_ref.shape
    grown = split2(jnp.exp(cum_ref[...]))
    square = jnp.zeros((rows, 1), F32)
    for j in range(parts):
        at = slice(j * lanes, (j + 1) * lanes)
        carried = jnp.dot(c_ref[...], state_ref[j], preferred_element_type=F32)
        factor = jnp.dot(
            grown, spread(heads, lanes, hsize, j * lanes), preferred_element_type=F32
        )
        y = y_ref[:, at] + factor * carried
        z = z_ref[:, at].astype(F32)
        value = y * (z / (1.0 + jnp.exp(-z)))
        gated[:, at] = value
        square = square + jnp.sum(value * value, axis=1, keepdims=True)
    scale = lax.rsqrt(square / width + 1e-05)
    for j in range(parts):
        at = slice(j * lanes, (j + 1) * lanes)
        out_ref[:, at] = (gated[:, at] * scale * gain_ref[:, at]).astype(BF)


def gated_norm(y, joined, cum, state, gain, row_tile, start, rows):
    width = y.shape[1]
    skip = start // row_tile
    heads, nstate = cum.shape[1], state.shape[1]
    at = 2 * width // nstate
    return pl.pallas_call(
        functools.partial(norm_kernel, width // heads),
        grid=(rows // row_tile,),
        in_specs=[
            pl.BlockSpec((row_tile, width), lambda i: (i + skip, 0)),
            pl.BlockSpec((row_tile, width), lambda i: (i + skip, 1)),
            pl.BlockSpec((row_tile, nstate), lambda i: (i + skip, at + 1)),
            pl.BlockSpec((row_tile, heads), lambda i: (i + skip, 0)),
            pl.BlockSpec(state.shape, lambda i: (0, 0, 0)),
            pl.BlockSpec((1, width), lambda i: (0, 0)),
        ],
        out_specs=pl.BlockSpec((row_tile, width), lambda i: (i, 0)),
        out_shape=jax.ShapeDtypeStruct((rows, width), BF),
        scratch_shapes=[pltpu.VMEM((row_tile, width), F32)],
        cost_estimate=pl.CostEstimate(
            flops=2 * rows * width * nstate,
            bytes_accessed=16 * rows * width,
            transcendentals=rows * width,
        ),
        compiler_params=params(),
        name="gated_norm",
    )(y, joined, joined, cum, state, gain)


def per_device(
    tokens_x, gate_z, in_b, in_c, log_decay, domain_ids, out_weight, norm_gain, skip_gain
):
    groups = lax.axis_size("dom")
    seq = lax.axis_size("seq")
    me = lax.axis_index("seq")
    rows, width = tokens_x.shape
    nstate = in_b.shape[1]
    heads = log_decay.shape[1]
    hsize = width // heads
    columns = out_weight.shape[2]

    ids = domain_ids.reshape(1, groups)
    order = jnp.sum(
        jnp.where(
            ids == jnp.arange(groups, dtype=jnp.int32)[:, None],
            jnp.arange(groups, dtype=jnp.int32)[None, :],
            0,
        ),
        axis=1,
    ).astype(jnp.int32)
    pad = jnp.zeros((rows, nstate - heads), log_decay.dtype)
    small = jnp.concatenate([in_b, in_c, log_decay, pad], axis=1)
    joined = lax.all_to_all(
        arrange(order, (tokens_x, gate_z, small), groups),
        "dom",
        split_axis=0,
        concat_axis=0,
        tiled=True,
    )

    half = columns // 2
    bits = [1 << i for i in range(seq.bit_length() - 1)]
    far = [bit for bit in bits if bit not in (1, PARTNER)]

    def far_pieces(block):
        found = {0: block}
        for bit in far:
            found.update({k | bit: exchange(v, "seq", bit) for k, v in list(found.items())})
        del found[0]
        return found

    def forward(found):
        return {k | 1: exchange(v, "seq", 1) for k, v in found.items()}

    own_a, own_b = out_weight[0, :, :half], out_weight[0, :, half:]
    far_a = far_pieces(own_a)
    near_a = exchange(own_a, "seq", 1)
    joined, near_a, far_a = lax.optimization_barrier((joined, near_a, far_a))
    forward_a = forward(far_a)

    ends, cum = block_states(joined, width, heads, nstate, seq)
    over = functools.partial(
        lax.all_to_all, axis_name="seq", split_axis=0, concat_axis=0, tiled=True
    )
    prefix = prefix_states(over(ends))
    prefix, far_own = lax.optimization_barrier((prefix, own_b))
    far_b = far_pieces(far_own)
    before = over(prefix)
    skip = jnp.repeat(skip_gain, hsize, axis=1)
    y = inner_part(joined, nstate, cum, skip)

    before, near_own = lax.optimization_barrier((before, own_b))
    near_b = exchange(near_own, "seq", 1)
    forward_b = forward(far_b)

    part = rows // 2
    first = gated_norm(y, joined, cum, before, norm_gain, 64, 0, part)
    theirs_first = exchange(first, "seq", PARTNER)
    second = gated_norm(y, joined, cum, before, norm_gain, 64, part, part)
    normed = jnp.concatenate([first, second], axis=0)
    theirs_second = exchange(second, "seq", PARTNER)

    early = [(0, {0: own_a, 1: near_a}), (half, {0: own_b}), (0, far_a)]
    late = [(0, forward_a), (half, {1: near_b}), (half, far_b)]
    last = [(half, forward_b)]

    def project(acts, piece):
        return jnp.dot(acts, piece, preferred_element_type=F32).astype(BF)

    def pieces_of(batch):
        return [(key, at, piece) for at, found in batch for key, piece in found.items()]

    out = jnp.zeros((rows, seq * columns), BF)
    for key, at, piece in pieces_of(early + late + last):
        out = lax.dynamic_update_slice(
            out, project(normed, piece), (0, (me ^ key) * columns + at)
        )
    returned = []
    for batch, halves in (
        (early, ((0, theirs_first),)),
        (early, ((part, theirs_second),)),
        (late, ((0, theirs_first),)),
        (late, ((part, theirs_second),)),
        (last, ((0, theirs_first), (part, theirs_second))),
    ):
        places, blocks = [], []
        for key, at, piece in pieces_of(batch):
            for start, acts in halves:
                places.append((start, key, at))
                blocks.append(project(acts, piece))
        returned.append((places, exchange(jnp.stack(blocks), "seq", PARTNER)))
    for places, block in returned:
        for i, (start, key, at) in enumerate(places):
            out = lax.dynamic_update_slice(
                out, block[i], (start, (me ^ (key | PARTNER)) * columns + at)
            )
    return out[None]


def solution(mesh):
    in_specs = (
        P(("dom", "seq"), None),
        P(("dom", "seq"), None),
        P(("dom", "seq"), None),
        P(("dom", "seq"), None),
        P(("dom", "seq"), None),
        P("dom", "seq", None),
        P("dom", None, "seq"),
        P("dom", None),
        P("dom", None),
    )
    return jax.shard_map(
        per_device, mesh=mesh, in_specs=in_specs, out_specs=P("dom", "seq", None), check_vma=False
    )
```
